32 devices in a mesh: grp: 2 (over y), seq: 4 (over z), head: 4 (over x, core).
Axes of the slice: x: 2, y: 2, z: 4, core: 2. Of those that a mesh axis runs over, the one named last changes fastest.
Arguments:
- queries: bfloat16 [5120, 8192], P(('grp', 'seq'), 'head'), parts along dimension 0, may hold values from -6 to 6
- keys: bfloat16 [5120, 8192], P(('grp', 'seq'), 'head'), parts along dimension 0, may hold values from -6 to 6
- values: bfloat16 [5120, 8192], P(('grp', 'seq'), 'head'), parts along dimension 0, may hold values from -40 to 40, as said below
- gain: float32 [8192], P('head'), may hold values from 0.5 to 1.5
- head_order: int32 [128], P('grp'), parts along dimension 0, may hold values from 0 to 63, each once
Outputs:
- attended: bfloat16 [5120, 8192], P(('grp', 'seq'), 'head'), parts along dimension 0
- final_state: float32 [128, 128, 128], P(('grp', 'seq'), 'head'), parts along dimension 0
The draws below stay inside these ranges and needn't reach their ends.
There are 2 independent parts, one for each index of `grp`. The reference program is written for one: setup_inputs(seed, part) draws one part's arguments, and reference() takes and returns one part's arrays. A program takes and returns all parts, laid end to end along the dimension named above; an argument that names none is the same for every part. Nothing has to cross between parts.
Inputs may be any that keep to these rules, and one draw needn't show every extreme that they name: `head_order`: each head appears exactly once. values of order one to some tens.
All inputs are finite; a program needn't handle non-finite values.
Results may differ from the reference program's by a relative error of at most 0.005.
Values sent between devices are 32-bit elements; how exact they have to be, the bound alone decides.
A program may use at most 128 MiB of HBM per device.

```python
import jax
import jax.numpy as jnp
from jax import lax

H = 64
DH = 128
TOK_DEV = 640
TOKENS = 2560
N_SEQ = 4


def draw_values(key, part):
    key_base = jax.random.fold_in(key, 11)
    key_rows = jax.random.fold_in(key, 12)
    key_cols = jax.random.fold_in(key, 13)
    shape = (TOKENS, H * DH)
    base = jnp.clip(jax.random.normal(key_base, shape, jnp.float32), -4.0, 4.0)
    row_scale = jnp.exp(jax.random.uniform(key_rows, (TOKENS, 1), jnp.float32, 0.0, 2.3))
    col_scale = jnp.exp(jax.random.uniform(key_cols, (1, H * DH), jnp.float32, -1.2, 1.2))
    return jnp.clip(base * row_scale * col_scale, -40.0, 40.0).astype(jnp.bfloat16)


def block_levels(key, extent, pieces, low, top_value):
    def one(axis_at, shards_of):
        steps = jax.random.uniform(jax.random.fold_in(jax.random.fold_in(key, 6), axis_at), (shards_of,), jnp.float32, low / len(pieces), top_value / len(pieces))
        return jnp.repeat(jnp.exp(steps), extent[axis_at] // shards_of).reshape((-1,) + (1,) * (len(extent) - axis_at - 1))

    loudness = one(*pieces[0])
    for cut in pieces[1:]:
        loudness = loudness * one(*cut)
    return loudness


def bell_draw(key, shape, scale, most, cuts=(), dtype=jnp.bfloat16):
    values = scale * jax.random.normal(key, shape, jnp.float32)
    if cuts:
        values = values * block_levels(key, shape, cuts, -0.22, 0.18)
    return jnp.clip(values, -most, most).astype(dtype)


def setup_inputs(seed: int = 0, part: int = 0) -> dict:
    streams_of = jax.random.split(jax.random.key(seed), 6)
    part_keys = jax.random.split(jax.random.fold_in(streams_of[5], part), 6)
    return {
        "queries": bell_draw(part_keys[0], (TOKENS, H * DH), 1.0, 6.0, ((0, 4), (1, 4))),
        "keys": bell_draw(part_keys[1], (TOKENS, H * DH), 1.0, 6.0, ((0, 4), (1, 4))),
        "values": draw_values(jax.random.fold_in(jax.random.fold_in(streams_of[5], part), 71), part),
        "gain": jnp.clip(1.0 + 0.1 * jax.random.normal(streams_of[3], (H * DH,), jnp.float32), 0.5, 1.5),
        "head_order": jax.random.permutation(part_keys[4], H).astype(jnp.int32),
    }


def reference(queries, keys, values, gain, head_order):
    q_all = queries.reshape(N_SEQ, TOK_DEV, H, DH)
    k_all = keys.reshape(N_SEQ, TOK_DEV, H, DH)
    v_all = values.reshape(N_SEQ, TOK_DEV, H, DH)
    gain_heads = gain.reshape(H, DH)
    causal = jnp.arange(TOK_DEV)[:, None] >= jnp.arange(TOK_DEV)[None, :]

    def step(carry, block):
        q_blk, k_blk, v_blk = block
        q32 = q_blk.astype(jnp.float32)
        k32 = k_blk.astype(jnp.float32)
        v32 = v_blk.astype(jnp.float32)
        local = jnp.einsum('thd,the->hde', k32, v32)
        prefix_low = carry.astype(jnp.bfloat16).astype(jnp.float32)
        scores = jnp.einsum('thd,uhd->htu', q32, k32)
        scores = jnp.where(causal[None], scores, 0.0).astype(jnp.bfloat16).astype(jnp.float32)
        mixed = jnp.einsum('htu,uhe->the', scores, v32) + jnp.einsum('thd,hde->the', q32, prefix_low)
        meansq = lax.optimization_barrier(jnp.mean(mixed * mixed, axis=-1, keepdims=True))
        normed = mixed / jnp.sqrt(meansq + 1e-06) * gain_heads[None]
        return (carry + local, normed.astype(jnp.bfloat16))
    start = jnp.zeros((H, DH, DH), jnp.float32)
    total_state, outs = lax.scan(step, start, (q_all, k_all, v_all))
    attended = outs.reshape(TOKENS, H * DH)
    final_state = jnp.take(total_state, head_order.astype(jnp.int32), axis=0)
    return (attended, final_state)
```

```python
import functools

import jax
import jax.numpy as jnp
from jax import lax
from jax.experimental import pallas as pl
from jax.experimental.pallas import tpu as pltpu
from jax.sharding import PartitionSpec as P

DH = 128
TILE = 256
EPS = 1e-06
MESH = pl.DeviceIdType.MESH


def dot(a, b, contract):
    return lax.dot_general(a, b, ((contract[:1], contract[1:]), ((), ())), preferred_element_type=jnp.float32)


def kernel(
    n_seq,
    n_head,
    q_hbm,
    k_hbm,
    v_hbm,
    gain_ref,
    order_ref,
    out_hbm,
    final_ref,
    q,
    k,
    v,
    mixed,
    att,
    block,
    up_in,
    up_out,
    down_in,
    down_out,
    total,
    rows,
    in_sem,
    out_sem,
    up_send,
    up_recv,
    down_send,
    down_recv,
    row_send,
    row_recv,
):
    heads, toks, _ = q.shape
    slots, part, _ = final_ref.shape
    s = lax.axis_index("seq")
    r = lax.axis_index("head")
    last = n_seq - 1
    upper = lax.rem(s + 1, n_seq)
    lower = lax.rem(s + last, n_seq)
    has_upper, has_lower = s < last, s > 0

    barrier = pltpu.get_barrier_semaphore()

    @pl.when(has_upper)
    def _():
        pl.semaphore_signal(barrier, inc=1, device_id={"seq": upper}, device_id_type=MESH)

    @pl.when(has_lower)
    def _():
        pl.semaphore_signal(barrier, inc=1, device_id={"seq": lower}, device_id_type=MESH)

    for d in range(1, n_head):
        pl.semaphore_signal(barrier, inc=1, device_id={"head": lax.rem(r + d, n_head)}, device_id_type=MESH)

    def load(i, h):
        hbm, vmem = ((k_hbm, k), (v_hbm, v), (q_hbm, q))[i]
        columns = pl.ds(pl.multiple_of(h * DH, DH), DH)
        return pltpu.make_async_copy(hbm.at[:, columns], vmem.at[h], in_sem.at[i, h])

    def store(h):
        columns = pl.ds(pl.multiple_of(h * DH, DH), DH)
        return pltpu.make_async_copy(att.at[h], out_hbm.at[:, columns], out_sem.at[h])

    def go_up(h):
        return pltpu.make_async_remote_copy(
            src_ref=up_out.at[h], dst_ref=up_in.at[h], send_sem=up_send.at[h], recv_sem=up_recv.at[h],
            device_id={"seq": upper}, device_id_type=MESH,
        )

    def go_down(h):
        return pltpu.make_async_remote_copy(
            src_ref=down_out.at[h], dst_ref=down_in.at[h], send_sem=down_send.at[h], recv_sem=down_recv.at[h],
            device_id={"seq": lower}, device_id_type=MESH,
        )

    def give_rows(d, h):
        peer = lax.rem(r + d, n_head)
        return pltpu.make_async_remote_copy(
            src_ref=total.at[h, pl.ds(pl.multiple_of(peer * part, part), part)],
            dst_ref=rows.at[r * heads + h],
            send_sem=row_send.at[d - 1, h], recv_sem=row_recv.at[d - 1, h],
            device_id={"head": peer}, device_id_type=MESH,
        )

    def start_loads(h, _):
        for i in range(3):
            load(i, h).start()
        return 0

    lax.fori_loop(0, heads, start_loads, 0)
    pl.semaphore_wait(barrier, n_head - 1 + has_upper.astype(jnp.int32) + has_lower.astype(jnp.int32))

    def step(t, _):
        @pl.when(t < heads)
        def _():
            load(0, t).wait()
            load(1, t).wait()
            block[t] = dot(k[t], v[t], (0, 0))

        c = t - s

        @pl.when((c >= 0) & (c < heads))
        def _():
            @pl.when(has_lower)
            def _():
                go_up(c).wait_recv()

            @pl.when(s == 0)
            def _():
                up_in[c] = jnp.zeros((DH, DH), jnp.float32)

            @pl.when(has_upper)
            def _():
                up_out[c] = up_in[c] + block[c]
                go_up(c).start()

        e = t - (last - s)

        @pl.when((e >= 0) & (e < heads))
        def _():
            @pl.when(has_upper)
            def _():
                go_down(e).wait_recv()

            @pl.when(s == last)
            def _():
                down_in[e] = jnp.zeros((DH, DH), jnp.float32)

            @pl.when(has_lower)
            def _():
                down_out[e] = down_in[e] + block[e]
                go_down(e).start()

        w = t - jnp.maximum(s, last - s)

        @pl.when((w >= 0) & (w < heads))
        def _():
            total[w] = up_in[w] + block[w] + down_in[w]
            for d in range(1, n_head):
                give_rows(d, w).start()
            rows[r * heads + w] = total[w, pl.ds(pl.multiple_of(r * part, part), part)]

        @pl.when(t < heads)
        def _():
            load(2, t).wait()
            for lo in range(0, toks, TILE):
                hi = min(lo + TILE, toks)
                q_rows = q[t, lo:hi]
                diag = dot(q_rows, k[t, lo:hi], (1, 1))
                row = lax.broadcasted_iota(jnp.int32, diag.shape, 0)
                col = lax.broadcasted_iota(jnp.int32, diag.shape, 1)
                diag = jnp.where(row >= col, diag, 0.0).astype(jnp.bfloat16)
                acc = dot(diag, v[t, lo:hi], (1, 0))
                if lo:
                    off = dot(q_rows, k[t, :lo], (1, 1)).astype(jnp.bfloat16)
                    acc = acc + dot(off, v[t, :lo], (1, 0))
                mixed[t, lo:hi] = acc

        @pl.when((c >= 0) & (c < heads))
        def _():
            prefix_low = up_in[c].astype(jnp.bfloat16)
            whole = mixed[c] + dot(q[c], prefix_low, (1, 0))
            meansq = jnp.mean(whole * whole, axis=-1, keepdims=True)
            gain = gain_ref[:, pl.ds(pl.multiple_of(c * DH, DH), DH)]
            att[c] = (whole * lax.rsqrt(meansq + EPS) * gain).astype(att.dtype)
            store(c).start()

        return 0

    lax.fori_loop(0, heads + last, step, 0)

    def arrive(h, _):
        for d in range(1, n_head):
            give_rows(d, h).wait_recv()
        return 0

    lax.fori_loop(0, heads, arrive, 0)

    def slot(j, _):
        final_ref[j] = rows[order_ref[s * slots + j]]
        return 0

    lax.fori_loop(0, slots, slot, 0)

    def finish(h, _):
        store(h).wait()

        @pl.when(has_upper)
        def _():
            go_up(h).wait_send()

        @pl.when(has_lower)
        def _():
            go_down(h).wait_send()

        for d in range(1, n_head):
            give_rows(d, h).wait_send()
        return 0

    lax.fori_loop(0, heads, finish, 0)


def on_device(n_seq, n_head, queries, keys, values, gain, head_order):
    toks, width = queries.shape
    heads = width // DH
    slots, part = head_order.shape[0] // n_seq, DH // n_head
    low = pltpu.VMEM((heads, toks, DH), jnp.bfloat16)
    state = pltpu.VMEM((heads, DH, DH), jnp.float32)
    sems = pltpu.SemaphoreType.DMA((heads,))
    peer_sems = pltpu.SemaphoreType.DMA((n_head - 1, heads))
    return pl.pallas_call(
        functools.partial(kernel, n_seq, n_head),
        out_shape=(
            jax.ShapeDtypeStruct((toks, width), jnp.bfloat16),
            jax.ShapeDtypeStruct((slots, part, DH), jnp.float32),
        ),
        in_specs=[pl.BlockSpec(memory_space=pl.ANY)] * 3
        + [pl.BlockSpec(memory_space=pltpu.VMEM), pl.BlockSpec(memory_space=pltpu.SMEM)],
        out_specs=(pl.BlockSpec(memory_space=pl.ANY), pl.BlockSpec(memory_space=pltpu.VMEM)),
        scratch_shapes=[
            low, low, low,
            pltpu.VMEM((heads, toks, DH), jnp.float32),
            low,
            state, state, state, state, state, state,
            pltpu.VMEM((heads * n_head, part, DH), jnp.float32),
            pltpu.SemaphoreType.DMA((3, heads)),
            sems, sems, sems, sems, sems,
            peer_sems, peer_sems,
        ],
        compiler_params=pltpu.CompilerParams(
            collective_id=0, has_side_effects=True, vmem_limit_bytes=48 * 2**20
        ),
        cost_estimate=pl.CostEstimate(
            flops=4 * toks * (toks + DH) * width, bytes_accessed=8 * toks * width, transcendentals=0
        ),
    )(queries, keys, values, gain.reshape(1, width), head_order)


def solution(mesh):
    return jax.shard_map(
        functools.partial(on_device, mesh.shape["seq"], mesh.shape["head"]),
        mesh=mesh,
        in_specs=(
            P(("grp", "seq"), "head"),
            P(("grp", "seq"), "head"),
            P(("grp", "seq"), "head"),
            P("head"),
            P("grp"),
        ),
        out_specs=(P(("grp", "seq"), "head"), P(("grp", "seq"), "head", None)),
        check_vma=False,
    )
```

```python
import functools

import jax
import jax.numpy as jnp
from jax import lax
from jax.experimental import pallas as pl
from jax.experimental.pallas import tpu as pltpu
from jax.sharding import PartitionSpec as P

DH = 128
TILE = 256
EPS = 1e-06
SKEW = 3
MESH = pl.DeviceIdType.MESH


def dot(a, b, contract):
    return lax.dot_general(a, b, ((contract[:1], contract[1:]), ((), ())), preferred_element_type=jnp.float32)


def kernel(
    n_seq,
    n_head,
    q_hbm,
    k_hbm,
    v_hbm,
    gain_ref,
    order_ref,
    out_hbm,
    final_ref,
    q,
    k,
    v,
    mixed,
    att,
    block,
    up_in,
    up_out,
    down_in,
    down_out,
    total,
    rows,
    in_sem,
    out_sem,
    up_send,
    up_recv,
    down_send,
    down_recv,
    row_send,
    row_recv,
):
    heads, toks, _ = q.shape
    slots, part, _ = final_ref.shape
    s = lax.axis_index("seq")
    r = lax.axis_index("head")
    last = n_seq - 1
    upper = lax.rem(s + 1, n_seq)
    lower = lax.rem(s + last, n_seq)
    has_upper, has_lower = s < last, s > 0

    barrier = pltpu.get_barrier_semaphore()

    @pl.when(has_upper)
    def _():
        pl.semaphore_signal(barrier, inc=1, device_id={"seq": upper}, device_id_type=MESH)

    @pl.when(has_lower)
    def _():
        pl.semaphore_signal(barrier, inc=1, device_id={"seq": lower}, device_id_type=MESH)

    for d in range(1, n_head):
        pl.semaphore_signal(barrier, inc=1, device_id={"head": lax.rem(r + d, n_head)}, device_id_type=MESH)

    def load(i, h):
        hbm, vmem = ((k_hbm, k), (v_hbm, v), (q_hbm, q))[i]
        columns = pl.ds(pl.multiple_of(h * DH, DH), DH)
        return pltpu.make_async_copy(hbm.at[:, columns], vmem.at[h], in_sem.at[i, h])

    def store(h):
        columns = pl.ds(pl.multiple_of(h * DH, DH), DH)
        return pltpu.make_async_copy(att.at[h], out_hbm.at[:, columns], out_sem.at[h])

    def go_up(h):
        return pltpu.make_async_remote_copy(
            src_ref=up_out.at[h], dst_ref=up_in.at[h], send_sem=up_send.at[h], recv_sem=up_recv.at[h],
            device_id={"seq": upper}, device_id_type=MESH,
        )

    def go_down(h):
        return pltpu.make_async_remote_copy(
            src_ref=down_out.at[h], dst_ref=down_in.at[h], send_sem=down_send.at[h], recv_sem=down_recv.at[h],
            device_id={"seq": lower}, device_id_type=MESH,
        )

    def give_rows(d, h):
        peer = lax.rem(r + d, n_head)
        return pltpu.make_async_remote_copy(
            src_ref=total.at[h, pl.ds(pl.multiple_of(peer * part, part), part)],
            dst_ref=rows.at[r * heads + h],
            send_sem=row_send.at[d - 1, h], recv_sem=row_recv.at[d - 1, h],
            device_id={"head": peer}, device_id_type=MESH,
        )

    def start_loads(h, _):
        for i in range(3):
            load(i, h).start()
        return 0

    lax.fori_loop(0, heads, start_loads, 0)
    pl.semaphore_wait(barrier, n_head - 1 + has_upper.astype(jnp.int32) + has_lower.astype(jnp.int32))

    def step(t, _):
        @pl.when(t < heads)
        def _():
            load(0, t).wait()
            load(1, t).wait()
            block[t] = dot(k[t], v[t], (0, 0))

        c = t - SKEW * s

        @pl.when((c >= 0) & (c < heads))
        def _():
            @pl.when(has_lower)
            def _():
                go_up(c).wait_recv()

            @pl.when(s == 0)
            def _():
                up_in[c] = jnp.zeros((DH, DH), jnp.float32)

            @pl.when(has_upper)
            def _():
                up_out[c] = up_in[c] + block[c]
                go_up(c).start()

        e = t - SKEW * (last - s)

        @pl.when((e >= 0) & (e < heads))
        def _():
            @pl.when(has_upper)
            def _():
                go_down(e).wait_recv()

            @pl.when(s == last)
            def _():
                down_in[e] = jnp.zeros((DH, DH), jnp.float32)

            @pl.when(has_lower)
            def _():
                down_out[e] = down_in[e] + block[e]
                go_down(e).start()

        w = t - SKEW * jnp.maximum(s, last - s)

        @pl.when((w >= 0) & (w < heads))
        def _():
            total[w] = up_in[w] + block[w] + down_in[w]
            for d in range(1, n_head):
                give_rows(d, w).start()
            rows[r * heads + w] = total[w, pl.ds(pl.multiple_of(r * part, part), part)]

        @pl.when(t < heads)
        def _():
            load(2, t).wait()
            for lo in range(0, toks, TILE):
                hi = min(lo + TILE, toks)
                q_rows = q[t, lo:hi]
                diag = dot(q_rows, k[t, lo:hi], (1, 1))
                row = lax.broadcasted_iota(jnp.int32, diag.shape, 0)
                col = lax.broadcasted_iota(jnp.int32, diag.shape, 1)
                diag = jnp.where(row >= col, diag, 0.0).astype(jnp.bfloat16)
                acc = dot(diag, v[t, lo:hi], (1, 0))
                if lo:
                    off = dot(q_rows, k[t, :lo], (1, 1)).astype(jnp.bfloat16)
                    acc = acc + dot(off, v[t, :lo], (1, 0))
                mixed[t, lo:hi] = acc

        @pl.when((c >= 0) & (c < heads))
        def _():
            prefix_low = up_in[c].astype(jnp.bfloat16)
            whole = mixed[c] + dot(q[c], prefix_low, (1, 0))
            meansq = jnp.mean(whole * whole, axis=-1, keepdims=True)
            gain = gain_ref[:, pl.ds(pl.multiple_of(c * DH, DH), DH)]
            att[c] = (whole * lax.rsqrt(meansq + EPS) * gain).astype(att.dtype)
            store(c).start()

        return 0

    lax.fori_loop(0, heads + SKEW * last, step, 0)

    def arrive(h, _):
        for d in range(1, n_head):
            give_rows(d, h).wait_recv()
        return 0

    lax.fori_loop(0, heads, arrive, 0)

    def slot(j, _):
        final_ref[j] = rows[order_ref[s * slots + j]]
        return 0

    lax.fori_loop(0, slots, slot, 0)

    def finish(h, _):
        store(h).wait()

        @pl.when(has_upper)
        def _():
            go_up(h).wait_send()

        @pl.when(has_lower)
        def _():
            go_down(h).wait_send()

        for d in range(1, n_head):
            give_rows(d, h).wait_send()
        return 0

    lax.fori_loop(0, heads, finish, 0)


def on_device(n_seq, n_head, queries, keys, values, gain, head_order):
    toks, width = queries.shape
    heads = width // DH
    slots, part = head_order.shape[0] // n_seq, DH // n_head
    low = pltpu.VMEM((heads, toks, DH), jnp.bfloat16)
    state = pltpu.VMEM((heads, DH, DH), jnp.float32)
    sems = pltpu.SemaphoreType.DMA((heads,))
    peer_sems = pltpu.SemaphoreType.DMA((n_head - 1, heads))
    return pl.pallas_call(
        functools.partial(kernel, n_seq, n_head),
        out_shape=(
            jax.ShapeDtypeStruct((toks, width), jnp.bfloat16),
            jax.ShapeDtypeStruct((slots, part, DH), jnp.float32),
        ),
        in_specs=[pl.BlockSpec(memory_space=pl.ANY)] * 3
        + [pl.BlockSpec(memory_space=pltpu.VMEM), pl.BlockSpec(memory_space=pltpu.SMEM)],
        out_specs=(pl.BlockSpec(memory_space=pl.ANY), pl.BlockSpec(memory_space=pltpu.VMEM)),
        scratch_shapes=[
            low, low, low,
            pltpu.VMEM((heads, toks, DH), jnp.float32),
            low,
            state, state, state, state, state, state,
            pltpu.VMEM((heads * n_head, part, DH), jnp.float32),
            pltpu.SemaphoreType.DMA((3, heads)),
            sems, sems, sems, sems, sems,
            peer_sems, peer_sems,
        ],
        compiler_params=pltpu.CompilerParams(
            collective_id=0, has_side_effects=True, vmem_limit_bytes=60 * 2**20
        ),
        cost_estimate=pl.CostEstimate(
            flops=4 * toks * (toks + DH) * width, bytes_accessed=8 * toks * width, transcendentals=0
        ),
    )(queries, keys, values, gain.reshape(1, width), head_order)


def solution(mesh):
    return jax.shard_map(
        functools.partial(on_device, mesh.shape["seq"], mesh.shape["head"]),
        mesh=mesh,
        in_specs=(
            P(("grp", "seq"), "head"),
            P(("grp", "seq"), "head"),
            P(("grp", "seq"), "head"),
            P("head"),
            P("grp"),
        ),
        out_specs=(P(("grp", "seq"), "head"), P(("grp", "seq"), "head", None)),
        check_vma=False,
    )
```

```python
import functools

import jax
import jax.numpy as jnp
from jax import lax
from jax.experimental import pallas as pl
from jax.experimental.pallas import tpu as pltpu
from jax.sharding import PartitionSpec as P

DH = 128
TILE = 256
EPS = 1e-06
SKEW = 3
AHEAD = 4
MESH = pl.DeviceIdType.MESH


def dot(a, b, contract):
    return lax.dot_general(a, b, ((contract[:1], contract[1:]), ((), ())), preferred_element_type=jnp.float32)


def kernel(
    n_seq,
    n_head,
    q_hbm,
    k_hbm,
    v_hbm,
    gain_hbm,
    order_hbm,
    out_ref,
    final_ref,
    q,
    k,
    v,
    mixed,
    block,
    up_in,
    up_out,
    down_in,
    down_out,
    total,
    rows,
    in_sem,
    up_send,
    up_recv,
    down_send,
    down_recv,
    row_send,
    row_recv,
    gain_ref,
    order_ref,
    side_sem,
):
    heads, toks, _ = q.shape
    slots, part, _ = final_ref.shape
    s = lax.axis_index("seq")
    r = lax.axis_index("head")
    last = n_seq - 1
    upper = lax.rem(s + 1, n_seq)
    lower = lax.rem(s + last, n_seq)
    has_upper, has_lower = s < last, s > 0

    barrier = pltpu.get_barrier_semaphore()

    @pl.when(has_upper)
    def _():
        pl.semaphore_signal(barrier, inc=1, device_id={"seq": upper}, device_id_type=MESH)

    @pl.when(has_lower)
    def _():
        pl.semaphore_signal(barrier, inc=1, device_id={"seq": lower}, device_id_type=MESH)

    for d in range(1, n_head):
        pl.semaphore_signal(barrier, inc=1, device_id={"head": lax.rem(r + d, n_head)}, device_id_type=MESH)

    def load(i, h):
        hbm, vmem = ((k_hbm, k), (v_hbm, v), (q_hbm, q))[i]
        columns = pl.ds(pl.multiple_of(h * DH, DH), DH)
        return pltpu.make_async_copy(hbm.at[:, columns], vmem.at[h], in_sem.at[i, h])

    def go_up(h):
        return pltpu.make_async_remote_copy(
            src_ref=up_out.at[h], dst_ref=up_in.at[h], send_sem=up_send.at[h], recv_sem=up_recv.at[h],
            device_id={"seq": upper}, device_id_type=MESH,
        )

    def go_down(h):
        return pltpu.make_async_remote_copy(
            src_ref=down_out.at[h], dst_ref=down_in.at[h], send_sem=down_send.at[h], recv_sem=down_recv.at[h],
            device_id={"seq": lower}, device_id_type=MESH,
        )

    def give_rows(d, h):
        peer = lax.rem(r + d, n_head)
        return pltpu.make_async_remote_copy(
            src_ref=total.at[h, pl.ds(pl.multiple_of(peer * part, part), part)],
            dst_ref=rows.at[r * heads + h],
            send_sem=row_send.at[d - 1, h], recv_sem=row_recv.at[d - 1, h],
            device_id={"head": peer}, device_id_type=MESH,
        )

    def start_loads(h, _):
        for i in range(3):
            load(i, h).start()
        return 0

    lax.fori_loop(0, min(AHEAD, heads), start_loads, 0)
    gain_copy = pltpu.make_async_copy(gain_hbm, gain_ref, side_sem.at[0])
    order_copy = pltpu.make_async_copy(order_hbm, order_ref, side_sem.at[1])
    gain_copy.start()
    order_copy.start()
    pl.semaphore_wait(barrier, n_head - 1 + has_upper.astype(jnp.int32) + has_lower.astype(jnp.int32))

    gain_copy.wait()

    def step(t, _):
        @pl.when(t < heads)
        def _():
            load(0, t).wait()
            load(1, t).wait()
            block[t] = dot(k[t], v[t], (0, 0))

        c = t - SKEW * s

        @pl.when((c >= 0) & (c < heads))
        def _():
            @pl.when(has_lower)
            def _():
                go_up(c).wait_recv()

            @pl.when(s == 0)
            def _():
                up_in[c] = jnp.zeros((DH, DH), jnp.float32)

            @pl.when(has_upper)
            def _():
                up_out[c] = up_in[c] + block[c]
                go_up(c).start()

        e = t - SKEW * (last - s)

        @pl.when((e >= 0) & (e < heads))
        def _():
            @pl.when(has_upper)
            def _():
                go_down(e).wait_recv()

            @pl.when(s == last)
            def _():
                down_in[e] = jnp.zeros((DH, DH), jnp.float32)

            @pl.when(has_lower)
            def _():
                down_out[e] = down_in[e] + block[e]
                go_down(e).start()

        w = t - SKEW * jnp.maximum(s, last - s)

        @pl.when((w >= 0) & (w < heads))
        def _():
            total[w] = up_in[w] + block[w] + down_in[w]
            for d in range(1, n_head):
                give_rows(d, w).start()
            rows[r * heads + w] = total[w, pl.ds(pl.multiple_of(r * part, part), part)]

        @pl.when(t + AHEAD < heads)
        def _():
            start_loads(t + AHEAD, 0)

        @pl.when(t < heads)
        def _():
            load(2, t).wait()
            for lo in range(0, toks, TILE):
                hi = min(lo + TILE, toks)
                q_rows = q[t, lo:hi]
                diag = dot(q_rows, k[t, lo:hi], (1, 1))
                row = lax.broadcasted_iota(jnp.int32, diag.shape, 0)
                col = lax.broadcasted_iota(jnp.int32, diag.shape, 1)
                diag = jnp.where(row >= col, diag, 0.0).astype(jnp.bfloat16)
                acc = dot(diag, v[t, lo:hi], (1, 0))
                if lo:
                    off = dot(q_rows, k[t, :lo], (1, 1)).astype(jnp.bfloat16)
                    acc = acc + dot(off, v[t, :lo], (1, 0))
                mixed[t, lo:hi] = acc

        @pl.when((c >= 0) & (c < heads))
        def _():
            prefix_low = up_in[c].astype(jnp.bfloat16)
            whole = mixed[c] + dot(q[c], prefix_low, (1, 0))
            meansq = jnp.mean(whole * whole, axis=-1, keepdims=True)
            columns = pl.ds(pl.multiple_of(c * DH, DH), DH)
            gain = gain_ref[:, columns]
            out_ref[:, columns] = (whole * lax.rsqrt(meansq + EPS) * gain).astype(out_ref.dtype)

        return 0

    lax.fori_loop(0, heads + SKEW * last, step, 0)

    def arrive(h, _):
        for d in range(1, n_head):
            give_rows(d, h).wait_recv()
        return 0

    lax.fori_loop(0, heads, arrive, 0)

    order_copy.wait()

    def slot(j, _):
        final_ref[j] = rows[order_ref[s * slots + j]]
        return 0

    lax.fori_loop(0, slots, slot, 0)

    def finish(h, _):
        @pl.when(has_upper)
        def _():
            go_up(h).wait_send()

        @pl.when(has_lower)
        def _():
            go_down(h).wait_send()

        for d in range(1, n_head):
            give_rows(d, h).wait_send()
        return 0

    lax.fori_loop(0, heads, finish, 0)


def on_device(n_seq, n_head, queries, keys, values, gain, head_order):
    toks, width = queries.shape
    heads = width // DH
    slots, part = head_order.shape[0] // n_seq, DH // n_head
    low = pltpu.VMEM((heads, toks, DH), jnp.bfloat16)
    state = pltpu.VMEM((heads, DH, DH), jnp.float32)
    sems = pltpu.SemaphoreType.DMA((heads,))
    peer_sems = pltpu.SemaphoreType.DMA((n_head - 1, heads))
    return pl.pallas_call(
        functools.partial(kernel, n_seq, n_head),
        out_shape=(
            jax.ShapeDtypeStruct((toks, width), jnp.bfloat16),
            jax.ShapeDtypeStruct((slots, part, DH), jnp.float32),
        ),
        in_specs=[pl.BlockSpec(memory_space=pltpu.HBM)] * 3
        + [pl.BlockSpec(memory_space=pltpu.HBM)] * 2,
        out_specs=(pl.BlockSpec(memory_space=pltpu.VMEM),) * 2,
        scratch_shapes=[
            low, low, low,
            pltpu.VMEM((heads, toks, DH), jnp.float32),
            state, state, state, state, state, state,
            pltpu.VMEM((heads * n_head, part, DH), jnp.float32),
            pltpu.SemaphoreType.DMA((3, heads)),
            sems, sems, sems, sems,
            peer_sems, peer_sems,
            pltpu.VMEM((1, width), jnp.float32),
            pltpu.SMEM(head_order.shape, jnp.int32),
            pltpu.SemaphoreType.DMA((2,)),
        ],
        compiler_params=pltpu.CompilerParams(
            collective_id=0, has_side_effects=True, vmem_limit_bytes=50 * 2**20
        ),
        cost_estimate=pl.CostEstimate(
            flops=4 * toks * (toks + DH) * width, bytes_accessed=8 * toks * width, transcendentals=0
        ),
    )(queries, keys, values, gain.reshape(1, width), head_order)


def solution(mesh):
    return jax.shard_map(
        functools.partial(on_device, mesh.shape["seq"], mesh.shape["head"]),
        mesh=mesh,
        in_specs=(
            P(("grp", "seq"), "head"),
            P(("grp", "seq"), "head"),
            P(("grp", "seq"), "head"),
            P("head"),
            P("grp"),
        ),
        out_specs=(P(("grp", "seq"), "head"), P(("grp", "seq"), "head", None)),
        check_vma=False,
    )
```
